512 devices in a mesh: seq: 128 (over z, x_lo, y), batch: 4 (over x_hi, core).
Axes of the slice: x: 4 (x_hi: 2, x_lo: 2; x = x_hi * 2 + x_lo), y: 8, z: 8, core: 2. Of those that a mesh axis runs over, the one named last changes fastest.
Arguments:
- coarse_act: bfloat16 [8, 8192, 1536], P('batch', 'seq'), may hold values from -6 to 6
- skip_act: bfloat16 [8, 16384, 1536], P('batch', 'seq'), may hold values from -6 to 6
- proj_in: bfloat16 [1536, 1536], P('seq'), may hold values from -0.15625 to 0.15625
- proj_out: bfloat16 [1536, 1536], P('seq'), may hold values from -0.15625 to 0.15625
- depth_kernel: float32 [3, 1536], replicated, may hold values from -3.5 to 3.5
- norm_gain: float32 [1536], replicated, may hold values from 0.5 to 1.5
- grad_out: bfloat16 [8, 16384, 1536], P('batch', 'seq'), may hold values from -6 to 6
Outputs:
- block_out: bfloat16 [8, 16384, 1536], P('batch', 'seq')
- grad_coarse_act: bfloat16 [8, 8192, 1536], P('batch', 'seq')
- grad_kernel: float32 [3, 1536], replicated
- grad_gain: float32 [1536], replicated
The draws below stay inside these ranges and needn't reach their ends.
All inputs are finite; a program needn't handle non-finite values.
Results may differ from the reference program's by a relative error of at most 0.012.
Values may be sent and summed in bfloat16 or wider, within the bound.
A program may use at most 128 MiB of HBM per device.

```python
import jax
import jax.numpy as jnp
from jax import lax

C = 1536
BINS = 16384
COARSE = 8192
SAMPLES = 8


def level_of(stream_key, shape, shards, least, largest):
    level = 1.0
    for position, shards_of in shards:
        steps = jax.random.uniform(jax.random.fold_in(jax.random.fold_in(stream_key, 6), position), (shards_of,), jnp.float32, least / len(shards), largest / len(shards))
        level = level * jnp.repeat(jnp.exp(steps), shape[position] // shards_of).reshape((-1,) + (1,) * (len(shape) - 1 - position))
    return level


def noise(key, extent, scale, limit, split=(), dtype=jnp.bfloat16):
    values = jax.random.normal(key, extent, jnp.float32) * scale
    if len(split) > 0:
        values = level_of(key, extent, split, -0.22, 0.18) * values
    return jnp.clip(values, min=-limit, max=limit).astype(dtype)


def setup_inputs(seed: int = 0) -> dict:
    splits = jax.random.split(jax.random.key(seed), 8)
    coarse_act = noise(splits[0], (SAMPLES, COARSE, C), 1.0, 6.0, ((0, 4), (1, 128)))
    skip_act = noise(splits[1], (SAMPLES, BINS, C), 1.0, 6.0, ((0, 4), (1, 128)))
    proj_in = noise(splits[2], (C, C), C ** -0.5, 0.15625, ((0, 128),))
    proj_out = noise(splits[3], (C, C), C ** -0.5, 0.15625, ((0, 128),))
    depth_kernel = noise(splits[4], (3, C), 3 ** -0.5, 3.5, (), jnp.float32)
    norm_gain = jnp.clip(1.0 + 0.1 * jax.random.normal(splits[5], (C,), jnp.float32), 0.5, 1.5)
    grad_out = noise(splits[6], (SAMPLES, BINS, C), 1.0, 6.0, ((0, 4), (1, 128)))
    return {"coarse_act": coarse_act, "skip_act": skip_act, "proj_in": proj_in, "proj_out": proj_out, "depth_kernel": depth_kernel, "norm_gain": norm_gain, "grad_out": grad_out}


epsilon = 1e-05

def norm_gelu(values_in, gain):
    values = values_in.astype(jnp.float32)
    average = lax.optimization_barrier(jnp.mean(values, axis=-1, keepdims=True))
    centered = values - average
    variance = lax.optimization_barrier(jnp.mean(centered * centered, axis=-1, keepdims=True))
    return jax.nn.gelu(centered * lax.rsqrt(variance + epsilon) * gain, approximate=False)

def one_sample(coarse_act, skip_act, grad_out, proj_in, proj_out, depth_kernel, norm_gain):
    activated = norm_gelu(coarse_act, norm_gain)
    act_low = activated.astype(jnp.bfloat16)
    coarse = jnp.dot(act_low, proj_in, preferred_element_type=jnp.float32).astype(jnp.bfloat16)
    merged = (jnp.repeat(coarse, 2, axis=0).astype(jnp.float32) + skip_act.astype(jnp.float32)).astype(jnp.bfloat16)
    padded = jnp.pad(merged, ((1, 1), (0, 0)))
    mixed = depth_kernel[0] * padded[:-2] + depth_kernel[1] * padded[1:-1] + depth_kernel[2] * padded[2:]
    mixed = mixed.astype(jnp.bfloat16)
    block_out = jnp.dot(mixed, proj_out, preferred_element_type=jnp.float32).astype(jnp.bfloat16)
    grad_mixed = jnp.dot(grad_out, proj_out.T, preferred_element_type=jnp.float32).astype(jnp.bfloat16)
    grad_wide = grad_mixed.astype(jnp.float32)
    grad_kernel = jnp.stack([lax.optimization_barrier(jnp.sum(padded[shift:shift + BINS].astype(jnp.float32) * grad_wide, axis=0)) for shift in range(3)])
    grad_pad = jnp.pad(grad_wide, ((1, 1), (0, 0)))
    grad_merged = depth_kernel[0] * grad_pad[2:] + depth_kernel[1] * grad_pad[1:-1] + depth_kernel[2] * grad_pad[:-2]
    grad_coarse = lax.optimization_barrier(jnp.sum(grad_merged.reshape(COARSE, 2, C), axis=1)).astype(jnp.bfloat16)
    grad_act = jnp.dot(grad_coarse, proj_in.T, preferred_element_type=jnp.float32)
    unused, pullback = jax.vjp(norm_gelu, coarse_act, norm_gain)
    grad_cur, grad_gain = pullback(grad_act)
    return (block_out, grad_cur.astype(jnp.bfloat16), grad_kernel, grad_gain)

def reference(coarse_act, skip_act, proj_in, proj_out, depth_kernel, norm_gain, grad_out):

    def step(items):
        return one_sample(items[0], items[1], items[2], proj_in, proj_out, depth_kernel, norm_gain)
    block_out, grad_cur, kernels, gains = lax.map(step, (coarse_act, skip_act, grad_out))
    return (block_out, grad_cur, lax.optimization_barrier(jnp.sum(kernels, axis=0)), lax.optimization_barrier(jnp.sum(gains, axis=0)))
```

```python
import functools
import jax
import jax.numpy as jnp
from jax import lax
from jax.experimental import pallas as pl
from jax.experimental.pallas import tpu as pltpu
from jax.sharding import Mesh
from jax.sharding import PartitionSpec as P

AXES = ("z", "xl", "y", "xh", "core")
F32 = jnp.float32
BF16 = jnp.bfloat16
C = 1536


def remote(src, dst, send, recv, dev):
    return pltpu.make_async_remote_copy(
        src_ref=src, dst_ref=dst, send_sem=send, recv_sem=recv,
        device_id=dev, device_id_type=pl.DeviceIdType.MESH)


def ds128(i, n=128):
    return pl.ds(pl.multiple_of(i, 128), n)


class Here:
    def __init__(self):
        for a in AXES:
            setattr(self, a, lax.axis_index(a))
        self.x = 2 * self.xh + self.xl
        self.quad = self.y // 4
        self.j = self.y % 4

    def on_x(self, step):
        x = (self.x + step + 4) % 4
        return {"xh": x // 2, "xl": x % 2}

    def along(self, core, first, step):
        name = "y" if (core == 0) == first else "z"
        return {name: (getattr(self, name) + step + 8) % 8}


def on_core(here, f):
    for c in (0, 1):
        @pl.when(here.core == c)
        def _(c=c):
            f(c)


def enter(here):
    barrier = pltpu.get_barrier_semaphore()
    peers = []
    for d in range(1, 8):
        peers.append({"y": (here.y + d) % 8})
        peers.append({"z": (here.z + d) % 8})
    for d in range(4):
        for e in range(2):
            if d or e:
                peers.append({**here.on_x(d), "core": (here.core + e) % 2})
    for step in (1, -1):
        for d in range(1, 4):
            peers.append({**here.on_x(step), "y": 4 * here.quad + (here.j + d) % 4})
    seq = here.z * 16 + here.xl * 8 + here.y
    for step in (1, 127):
        n = (seq + step) % 128
        peers.append({"z": n // 16, "xl": n % 16 // 8, "y": n % 8})
    for p in peers:
        pl.semaphore_signal(barrier, inc=1, device_id=p, device_id_type=pl.DeviceIdType.MESH)
    pl.semaphore_wait(barrier, len(peers))


class Weights:
    def __init__(self, here, w, stage, queue, queue0, s0, r0, sx0, rx0, s1, r1, s2, r2, s3, r3, s4, r4):
        self.__dict__.update(locals())

    def block(self, k, t, xl, z, y):
        return self.w.at[k, z, xl, y // 4, :, ds128(512 * t + 128 * (y % 4))]

    def own(self, c, k, cls, step=0):
        h = self.here
        t, xl = (0, c) if cls == 0 else (1 + c, h.xl)
        y, z = (((h.y + step + 8) % 8, h.z) if c == 0 else (h.y, (h.z + step + 8) % 8))
        return self.block(k, t, xl, z, y)

    def chunk(self, c, k, cls, step, other=False):
        h = self.here
        t, xl = (0, c) if cls == 0 else (1 + c, (1 - h.xl) if other else h.xl)
        if c == 0:
            return self.w.at[k, (h.z + step + 8) % 8, xl, :, :, pl.ds(512 * t, 512)]
        y = (h.y + step + 8) % 8
        return self.w.at[k, :, xl, y // 4, :, ds128(512 * t + 128 * (y % 4))]

    def chunks(self, k, n):
        return self.w.at[k, pl.ds(0, n), 0, :, :, pl.ds(0, 512)]

    def pack(self, w_in, w_out):
        h = self.here
        for k, ref in enumerate((w_in, w_out)):
            for j in range(4):
                self.stage[j, k, 12:16, :] = jnp.zeros((4, 256), BF16)
                self.stage[j, k, 0:12, 0:128] = ref[:, 128 * j : 128 * j + 128]
                self.stage[j, k, 0:12, 128:256] = ref[:, ds128(512 * (1 + h.core) + 128 * j)]

    def swap_copies(self):
        h = self.here
        out = []
        for d in range(1, 4):
            j = (h.j + d) % 4
            out.append(remote(self.stage.at[j], self.queue.at[h.j], self.s0.at[d], self.r0.at[d],
                              {"y": 4 * h.quad + j}))
        for d in range(4):
            j = (h.j + d) % 4
            out.append(remote(self.stage.at[j, :, :, pl.ds(0, 128)], self.queue0.at[h.j], self.sx0.at[d],
                              self.rx0.at[d], {**h.on_x(1), "y": 4 * h.quad + j}))
        return out

    def swap_start(self):
        self.queue[self.here.j] = self.stage[self.here.j]
        for c in self.swap_copies():
            c.start()

    def swap_finish(self):
        h = self.here
        for c in self.swap_copies():
            c.wait()
        row = lax.broadcasted_iota(jnp.int32, (48, 64), 0)
        col = lax.broadcasted_iota(jnp.int32, (48, 64), 1)
        pick = ((row // 12 == col // 16) & (row % 12 == col % 16)).astype(BF16)
        for k in (0, 1):
            mine = self.queue[:, k].reshape(64, 256)
            first = jnp.where(h.xl == h.core, mine[:, :128].astype(F32),
                              self.queue0[:, k].reshape(64, 128).astype(F32)).astype(BF16)
            self.w[k, h.z, h.core, h.quad, :, ds128(128 * h.j)] = jnp.dot(
                pick, first, preferred_element_type=F32).astype(BF16)
            self.w[k, h.z, h.xl, h.quad, :, ds128(512 * (1 + h.core) + 128 * h.j)] = jnp.dot(
                pick, mine[:, 128:], preferred_element_type=F32).astype(BF16)

    def first_start(self, c, k):
        for cls in (1, 0):
            for d in (1, 7, 2, 6, 3, 5, 4):
                src = self.own(c, k, cls)
                remote(src, src, self.s1.at[k, cls], self.r1.at[k, cls], self.here.along(c, True, d)).start()

    def seven(self, k):
        return self.w.at[k, pl.ds(0, 7), 0, 0, :, pl.ds(0, 128)]

    def first_wait(self, c, k, cls):
        ref = self.seven(k)
        remote(ref, ref, self.s1.at[k, cls], self.r1.at[k, cls], self.here.along(c, True, 1)).wait_recv()

    def to_core(self, c, k, which, step):
        src = self.chunk(c, k, min(which, 1), step, which == 2)
        remote(src, src, self.s4.at[k, which], self.r4.at[k, which], {"core": 1 - c}).start()

    def hop(self, c, k, cls, step):
        src = self.chunk(c, k, cls, step)
        far = 4 if cls == 1 else 3
        dirs = []
        if step <= 0 and 1 - step <= far:
            dirs.append((1, 1 - step))
        if step >= 0 and 1 + step <= 7 - far:
            dirs.append((-1, 1 + step))
        for way, nth in dirs:
            n = 0 if way == 1 else 1
            remote(src, src, self.s2.at[k, cls, n], self.r2.at[k, cls, n, nth],
                   self.here.along(c, False, way)).start()
        if cls == 1:
            far_x = 1 if step < 0 else -1
            remote(src, src, self.s3.at[k], self.r3.at[k, step % 8], self.here.on_x(far_x)).start()
        self.to_core(c, k, cls, step)

    def second_start(self, c, k):
        for cls in (1, 0):
            self.first_wait(c, k, cls)
            self.hop(c, k, cls, 0)

    def second_step(self, c, k, nth):
        for cls in (1, 0):
            far = 4 if cls == 1 else 3
            for way in (1, -1):
                if nth > (far if way == 1 else 7 - far):
                    continue
                n = 0 if way == 1 else 1
                src = self.chunk(c, k, cls, -nth * way)
                remote(src, src, self.s2.at[k, cls, n], self.r2.at[k, cls, n, nth],
                       self.here.along(c, False, way)).wait_recv()
                self.hop(c, k, cls, -nth * way)
        self.cross_x(c, k, nth - 1)

    def cross_x(self, c, k, nth):
        for step in ((0,) if nth == 0 else (nth, -nth) if nth < 4 else (-4,)):
            src = self.chunk(c, k, 1, step, True)
            remote(src, src, self.s3.at[k], self.r3.at[k, step % 8], self.here.on_x(1)).wait_recv()
            self.to_core(c, k, 2, step)

    def ready(self, c, k):
        ref = self.chunks(k, 8)
        for which in range(3):
            remote(ref, ref, self.s4.at[k, which], self.r4.at[k, which], {"core": 1 - c}).wait_recv()

    def sent(self, c, k):
        h = self.here
        for cls in range(2):
            ref = self.seven(k)
            remote(ref, ref, self.s1.at[k, cls], self.r1.at[k, cls], h.along(c, True, 1)).wait_send()
            far = 4 if cls == 1 else 3
            for n in range(2):
                ref = self.chunks(k, far if n == 0 else 7 - far)
                remote(ref, ref, self.s2.at[k, cls, n], self.r2.at[k, cls, n, 1], h.along(c, False, 1)).wait_send()
        ref = self.chunks(k, 8)
        remote(ref, ref, self.s3.at[k], self.r3.at[k, 0], h.on_x(1)).wait_send()
        for which in range(3):
            remote(ref, ref, self.s4.at[k, which], self.r4.at[k, which], {"core": 1 - c}).wait_send()

    def plan(self):
        return [
            [lambda c: self.first_start(c, 0), lambda c: self.first_start(c, 1)],
            [lambda c: self.second_start(c, 0)],
            [lambda c: self.second_step(c, 0, 1)],
            [lambda c: self.second_step(c, 0, 2), lambda c: self.second_start(c, 1)],
            [lambda c: self.second_step(c, 0, 3), lambda c: self.second_step(c, 1, 1)],
            [lambda c: self.second_step(c, 0, 4), lambda c: self.cross_x(c, 0, 4)],
            [lambda c: self.second_step(c, 1, 2)],
            [lambda c: self.second_step(c, 1, 3)],
            [lambda c: self.second_step(c, 1, 4), lambda c: self.cross_x(c, 1, 4)],
        ]


def weight_scratch():
    sem = pltpu.SemaphoreType.DMA
    return [
        pltpu.VMEM((2, 8, 2, 2, 48, C), BF16),
        pltpu.VMEM((4, 2, 16, 256), BF16),
        pltpu.VMEM((4, 2, 16, 256), BF16),
        pltpu.VMEM((4, 2, 16, 128), BF16),
        sem((4,)), sem((4,)), sem((4,)), sem((4,)),
        sem((2, 2)), sem((2, 2)),
        sem((2, 2, 2)), sem((2, 2, 2, 5)),
        sem((2,)), sem((2, 8)),
        sem((2, 3)), sem((2, 3)),
    ]


EPS = 1e-05
ROWS = 128


class Sum:
    def __init__(self, here, parts, got, send, recv):
        self.__dict__.update(locals())
        self.me = 2 * here.x + here.core

    def group(self, m):
        x = m // 2
        return {"xh": x // 2, "xl": x % 2, "core": m % 2}

    def copies(self, stage):
        h, out = self.here, []
        for d in range(1, 8):
            if stage in (0, 3):
                m = (self.me + d) % 8
                src = self.parts.at[stage, m if stage == 0 else 0]
                dst, to = self.got.at[stage, self.me], self.group(m)
            elif stage == 1:
                src, dst, to = self.parts.at[1, 0], self.got.at[1, h.y], {"y": (h.y + d) % 8}
            else:
                src, dst, to = self.parts.at[2, 0], self.got.at[2, h.z], {"z": (h.z + d) % 8}
            out.append(remote(src, dst, self.send.at[stage, d], self.recv.at[stage, d], to))
        return out

    def mine(self, stage):
        return self.here.y if stage == 1 else self.here.z if stage == 2 else self.me

    def start(self, stage):
        src = self.parts[0, self.me] if stage == 0 else self.parts[stage, 0]
        self.got[stage, self.mine(stage)] = src
        for c in self.copies(stage):
            c.start()

    def finish(self, stage):
        for c in self.copies(stage):
            c.wait()
        if stage < 3:
            total = self.got[stage, 0]
            for n in range(1, 8):
                total = total + self.got[stage, n]
            self.parts[stage + 1, 0] = total


def sum_scratch():
    sem = pltpu.SemaphoreType.DMA
    return [pltpu.VMEM((4, 8, 8, 128), F32), pltpu.VMEM((4, 8, 8, 128), F32), sem((4, 8)), sem((4, 8))]


def picked(rows, cols, where):
    r = lax.broadcasted_iota(jnp.int32, (rows, cols), 0)
    c = lax.broadcasted_iota(jnp.int32, (rows, cols), 1)
    return where(r, c).astype(BF16)


def dot(a, b):
    return jnp.dot(a, b, preferred_element_type=F32)


def dot_t(a, b):
    return lax.dot_general(a, b, (((1,), (1,)), ((), ())), preferred_element_type=F32)


def before(x, first):
    row = lax.broadcasted_iota(jnp.int32, x.shape, 0)
    return jnp.where(row == 0, first, pltpu.roll(x, 1, 0))


def after(x, last):
    row = lax.broadcasted_iota(jnp.int32, x.shape, 0)
    return jnp.where(row == x.shape[0] - 1, last, pltpu.roll(x, x.shape[0] - 1, 0))


def kernel(coarse_hbm, skip_hbm, w_in, w_out, taps, gain, grad_hbm, block_hbm, dx_hbm, gk_out, gg_out, *scratch):
    (ca, sk, go, halo_out, halo_in, act, gp, skp, halo, nrm, dgelu, scale, gm, gc, mer, mix, dn, dx, bo, part,
     in_sem, out_sem, hs, hr) = scratch[:24]
    here = Here()
    w = Weights(here, *scratch[24:40])
    total = Sum(here, *scratch[40:])
    seq = here.z * 16 + here.xl * 8 + here.y

    loads = [pltpu.make_async_copy(a, b, in_sem.at[n])
             for n, (a, b) in enumerate(((coarse_hbm, ca), (skip_hbm, sk), (grad_hbm, go)))]
    for c in loads:
        c.start()
    w.pack(w_out, w_in)
    enter(here)
    w.swap_start()

    for c in loads:
        c.wait()
    row = lax.broadcasted_iota(jnp.int32, (16, C), 0)
    for side in (0, 1):
        rows = jnp.zeros((16, C), F32)
        for n, (ref, last) in enumerate(((ca, 63), (sk, 127), (go, 127))):
            for s in (0, 1):
                if side == 0:
                    r = ref[s, last - 15 : last + 1, :].astype(F32)[15:16]
                else:
                    r = ref[s, 0:16, :].astype(F32)[0:1]
                rows = jnp.where(row == 4 * n + 2 * side + s, r, rows)
        halo_out[side] = rows.astype(BF16)

    def neighbour(step):
        s = (seq + step + 128) % 128
        return {"z": s // 16, "xl": s % 16 // 8, "y": s % 8}

    halos = [remote(halo_out.at[0], halo_in.at[0], hs.at[0], hr.at[0], neighbour(1)),
             remote(halo_out.at[1], halo_in.at[1], hs.at[1], hr.at[1], neighbour(-1))]
    for c in halos:
        c.start()

    w.swap_finish()
    on_core(here, lambda c: w.first_start(c, 0))
    on_core(here, lambda c: w.first_start(c, 1))

    def norm(x):
        x = x.astype(F32)
        centered = x - jnp.mean(x, axis=-1, keepdims=True)
        r = lax.rsqrt(jnp.mean(centered * centered, axis=-1, keepdims=True) + EPS)
        n = centered * r
        u = n * gain[...]
        half = 0.5 + 0.5 * lax.erf(u * 0.7071067811865476)
        return n, r, u, half

    def norm_rows(i):
        at = pl.ds(pl.multiple_of(16 * i, 16), 16)
        n, r, u, half = norm(ca[i // 4, pl.ds(pl.multiple_of(16 * (i % 4), 16), 16), :])
        nrm[at, :] = n
        scale[at, :] = jnp.broadcast_to(r, (16, 128))
        act[at, :] = (u * half).astype(BF16)
        dgelu[at, :] = half + u * (0.3989422804014327 * jnp.exp(-0.5 * u * u))

    lax.fori_loop(0, 4, lambda i, v: (norm_rows(i), v)[1], 0)
    for k in (0, 1):
        on_core(here, lambda c: w.second_start(c, k))
    lax.fori_loop(4, 8, lambda i, v: (norm_rows(i), v)[1], 0)

    for c in halos:
        c.wait()
    left = jnp.where(seq > 0, halo_in[0].astype(F32), 0.0)
    right = jnp.where(seq < 127, halo_in[1].astype(F32), 0.0)
    halo[...] = (left + right).astype(BF16)
    gp[256:272, :] = halo[...]
    on_core(here, lambda c: w.second_step(c, 0, 1))
    on_core(here, lambda c: w.second_step(c, 1, 1))
    _, _, u, half = norm(halo[...])
    act[128:144, :] = (u * half).astype(BF16)
    split = picked(128, 128, lambda r, c: c == 2 * (r % 64) + r // 64)
    for s in (0, 1):
        gp[128 * s : 128 * s + 128, :] = dot(split, go[s]).astype(BF16)
        skp[128 * s : 128 * s + 128, :] = dot(split, sk[s]).astype(BF16)
    on_core(here, lambda c: w.second_step(c, 0, 2))
    on_core(here, lambda c: w.second_step(c, 1, 2))
    on_core(here, lambda c: w.second_step(c, 0, 3))
    on_core(here, lambda c: w.second_step(c, 1, 3))
    on_core(here, lambda c: w.second_step(c, 0, 4))
    on_core(here, lambda c: w.cross_x(c, 0, 4))
    on_core(here, lambda c: w.second_step(c, 1, 4))
    on_core(here, lambda c: w.ready(c, 0))

    def cols(n):
        return ds128(384 * n, 384)

    def back(n):
        at = cols(n)
        rows = w.w[0, pl.ds(2 * n, 2)].reshape(384, C)
        gm[:, at] = dot_t(gp[...], rows).astype(BF16)
        t0, t1, t2 = (taps[t : t + 1, at] for t in range(3))
        edge = gm[256:272, at].astype(F32)
        for s in (0, 1):
            e = gm[128 * s : 128 * s + 64, at].astype(F32)
            o = gm[128 * s + 64 : 128 * s + 128, at].astype(F32)
            e1 = after(e, edge[10 + s : 11 + s])
            o1 = before(o, edge[8 + s : 9 + s])
            gc[64 * s : 64 * s + 64, at] = (t0 * (o + e1) + t1 * (e + o) + t2 * (o1 + e)).astype(BF16)

    lax.fori_loop(0, 2, lambda n, v: (back(n), v)[1], 0)
    on_core(here, lambda c: w.cross_x(c, 1, 4))
    lax.fori_loop(2, 4, lambda n, v: (back(n), v)[1], 0)
    on_core(here, lambda c: w.ready(c, 1))

    def forth(n):
        at = cols(n)
        co = dot(act[...], w.w[1, :, :, :, :, at].reshape(C, 384)).astype(BF16).astype(F32)
        t0, t1, t2 = (taps[t : t + 1, at] for t in range(3))
        skip_edge = halo[:, at].astype(F32)
        sums = [0.0, 0.0, 0.0]
        for s in (0, 1):
            c = co[64 * s : 64 * s + 64]
            me = (c + skp[128 * s : 128 * s + 64, at].astype(F32)).astype(BF16).astype(F32)
            mo = (c + skp[128 * s + 64 : 128 * s + 128, at].astype(F32)).astype(BF16).astype(F32)
            lo = (co[128 + s : 129 + s] + skip_edge[4 + s : 5 + s]).astype(BF16).astype(F32)
            hi = (co[130 + s : 131 + s] + skip_edge[6 + s : 7 + s]).astype(BF16).astype(F32)
            mo1 = before(mo, lo)
            me1 = after(me, hi)
            mix[128 * s : 128 * s + 64, at] = (t0 * mo1 + t1 * me + t2 * mo).astype(BF16)
            mix[128 * s + 64 : 128 * s + 128, at] = (t0 * me + t1 * mo + t2 * me1).astype(BF16)
            e = gm[128 * s : 128 * s + 64, at].astype(F32)
            o = gm[128 * s + 64 : 128 * s + 128, at].astype(F32)
            for t, v in enumerate((mo1 * e + me * o, me * e + mo * o, mo * e + me1 * o)):
                sums[t] = sums[t] + jnp.sum(v, axis=0, keepdims=True)
        for t in range(3):
            part[t : t + 1, at] = sums[t]

    lax.fori_loop(0, 4, lambda n, v: (forth(n), v)[1], 0)

    def gains(n, sums):
        at = cols(n)
        ga = dot_t(gc[...], w.w[1, pl.ds(2 * n, 2)].reshape(384, C))
        gu = ga * dgelu[:, at]
        nn = nrm[:, at]
        part[3:4, at] = jnp.sum(gu * nn, axis=0, keepdims=True)
        d = gu * gain[:, at]
        dn[:, at] = d
        return (sums[0] + jnp.sum(d, axis=1, keepdims=True), sums[1] + jnp.sum(d * nn, axis=1, keepdims=True))

    zero = jnp.zeros((ROWS, 1), F32)
    d_sum, dn_sum = lax.fori_loop(0, 4, gains, (zero, zero))

    for m in range(8):
        for i in range(6):
            total.parts[0, m, i : i + 1, :] = part[m // 2 : m // 2 + 1, 768 * (m % 2) + 128 * i : 768 * (m % 2) + 128 * i + 128]
        total.parts[0, m, 6:8, :] = jnp.zeros((2, 128), F32)
    total.start(0)

    d_mean, dn_mean = d_sum / C, dn_sum / C
    for n in range(4):
        at = pl.ds(384 * n, 384)
        v = scale[:, 0:1] * (dn[:, at] - d_mean - nrm[:, at] * dn_mean)
        dx[:, at] = v.astype(BF16)
    outs = [pltpu.make_async_copy(dx.at[pl.ds(64 * s, 64)], dx_hbm.at[s], out_sem.at[s]) for s in (0, 1)]
    for c in outs:
        c.start()
    total.finish(0)
    total.start(1)
    join = picked(128, 128, lambda r, c: r == 2 * (c % 64) + c // 64)
    for s in (0, 1):
        mer[128 * s : 128 * s + 128, :] = dot(join, mix[128 * s : 128 * s + 128, :]).astype(BF16)

    def final(n):
        at = cols(n)
        bo[:, at] = dot(mer[...], w.w[0, :, :, :, :, at].reshape(C, 384)).astype(BF16)

    lax.fori_loop(0, 2, lambda n, v: (final(n), v)[1], 0)
    total.finish(1)
    total.start(2)
    lax.fori_loop(2, 4, lambda n, v: (final(n), v)[1], 0)
    more = [pltpu.make_async_copy(bo.at[pl.ds(128 * s, 128)], block_hbm.at[s], out_sem.at[2 + s]) for s in (0, 1)]
    for c in more:
        c.start()
    total.finish(2)
    total.start(3)
    for k in (0, 1):
        on_core(here, lambda c: w.sent(c, k))
    for c in outs + more:
        c.wait()
    total.finish(3)
    for m in range(8):
        r, at = m // 2, 768 * (m % 2)
        for i in range(6):
            v = total.got[3, m, i : i + 1, :]
            if r < 3:
                gk_out[r : r + 1, at + 128 * i : at + 128 * i + 128] = v
            else:
                gg_out[0:1, at + 128 * i : at + 128 * i + 128] = v


def on_device(coarse_act, skip_act, proj_in, proj_out, depth_kernel, norm_gain, grad_out):
    vmem = pl.BlockSpec(memory_space=pltpu.VMEM)
    hbm = pl.BlockSpec(memory_space=pl.ANY)
    sem = pltpu.SemaphoreType.DMA

    def b(*shape):
        return pltpu.VMEM(shape, BF16)

    def f(*shape):
        return pltpu.VMEM(shape, F32)

    scratch = [
        b(2, 64, C), b(2, 128, C), b(2, 128, C), b(2, 16, C), b(2, 16, C), b(144, C), b(272, C), b(256, C), b(16, C),
        f(ROWS, C), f(ROWS, C), f(ROWS, 128), b(272, C), b(ROWS, C), b(256, C), b(256, C), f(ROWS, C), b(ROWS, C),
        b(256, C), f(8, C), sem((3,)), sem((4,)), sem((2,)), sem((2,)),
    ] + weight_scratch() + sum_scratch()
    block, dx, gk, gg = pl.pallas_call(
        kernel,
        out_shape=(
            jax.ShapeDtypeStruct((2, 128, C), BF16), jax.ShapeDtypeStruct((2, 64, C), BF16),
            jax.ShapeDtypeStruct((3, C), F32), jax.ShapeDtypeStruct((1, C), F32)),
        in_specs=[hbm, hbm, vmem, vmem, vmem, vmem, hbm],
        out_specs=(hbm, hbm, vmem, vmem),
        scratch_shapes=scratch,
        compiler_params=pltpu.CompilerParams(collective_id=0, has_side_effects=True, vmem_limit_bytes=48 << 20),
        cost_estimate=pl.CostEstimate(flops=3700000000, bytes_accessed=4000000, transcendentals=400000),
    )(coarse_act, skip_act, proj_in, proj_out, depth_kernel, norm_gain.reshape(1, C), grad_out)
    return block, dx, gk, gg.reshape(C)


def solution(mesh):
    split = Mesh(mesh.devices.reshape(8, 2, 8, 2, 2), AXES)
    seq, batch = ("z", "xl", "y"), ("xh", "core")
    big, rows = P(batch, seq, None), P(seq, None)
    return jax.shard_map(
        on_device, mesh=split, in_specs=(big, big, rows, rows, P(), P(), big),
        out_specs=(big, big, P(), P()), check_vma=False)
```

```python
import functools
import jax
import jax.numpy as jnp
from jax import lax
from jax.experimental import pallas as pl
from jax.experimental.pallas import tpu as pltpu
from jax.sharding import Mesh
from jax.sharding import PartitionSpec as P

AXES = ("z", "xl", "y", "xh", "core")
F32 = jnp.float32
BF16 = jnp.bfloat16
C = 1536


def remote(src, dst, send, recv, dev):
    return pltpu.make_async_remote_copy(
        src_ref=src, dst_ref=dst, send_sem=send, recv_sem=recv,
        device_id=dev, device_id_type=pl.DeviceIdType.MESH)


def ds128(i, n=128):
    return pl.ds(pl.multiple_of(i, 128), n)


class Here:
    def __init__(self):
        for a in AXES:
            setattr(self, a, lax.axis_index(a))
        self.x = 2 * self.xh + self.xl

    def on_x(self, step):
        x = (self.x + step + 4) % 4
        return {"xh": x // 2, "xl": x % 2}

    def along(self, core, step):
        name = "z" if core == 0 else "y"
        return {name: (getattr(self, name) + step + 8) % 8}


def on_core(here, f):
    for c in (0, 1):
        @pl.when(here.core == c)
        def _(c=c):
            f(c)


def enter(here):
    barrier = pltpu.get_barrier_semaphore()
    peers = []
    for d in range(1, 8):
        peers.append({"y": (here.y + d) % 8})
        peers.append({"z": (here.z + d) % 8})
        for step in (1, -1):
            peers.append({**here.on_x(step), "y": (here.y + d * (1 - here.core)) % 8, "z": (here.z + d * here.core) % 8})
    for d in range(4):
        for e in range(2):
            if d or e:
                peers.append({**here.on_x(d), "core": (here.core + e) % 2})
    seq = here.z * 16 + here.xl * 8 + here.y
    for step in (1, 127):
        n = (seq + step) % 128
        peers.append({"z": n // 16, "xl": n % 16 // 8, "y": n % 8})
    for p in peers:
        pl.semaphore_signal(barrier, inc=1, device_id=p, device_id_type=pl.DeviceIdType.MESH)
    pl.semaphore_wait(barrier, len(peers))


class Weights:
    def __init__(self, here, w, wp, s1, r1, s1x, s2, r2, s3, r3, s4, r4):
        self.__dict__.update(locals())

    def own(self, k, cls):
        h = self.here
        t = 1 + h.core if cls else 0
        return self.wp.at[k, h.z, h.xl, h.y, :, ds128(384 * t, 384)]

    def chunk(self, c, k, cls, step, other=False):
        h = self.here
        t, xl = (0, c) if cls == 0 else (1 + c, (1 - h.xl) if other else h.xl)
        at = pl.ds(384 * t, 384)
        if c == 0:
            return self.wp.at[k, (h.z + step + 8) % 8, xl, :, :, at]
        return self.wp.at[k, :, xl, (h.y + step + 8) % 8, :, at]

    def chunks(self, k, n):
        return self.wp.at[k, pl.ds(0, n), 0, :, :, pl.ds(0, 384)]

    def blocks(self, k, n):
        return self.wp.at[k, pl.ds(0, n), 0, 0, :, pl.ds(0, 384)]

    def pack(self, *refs):
        h = self.here
        for k, ref in enumerate(refs):
            v = ref[...].astype(F32)
            for t in range(3):
                e = v[:, 512 * t + 384 : 512 * t + 512]
                low = jnp.concatenate([e[0:4], e[4:8], e[8:12]], axis=1)
                both = jnp.concatenate([v[:, 512 * t : 512 * t + 384], low], axis=0)
                self.wp[k, h.z, h.xl, h.y, :, 384 * t : 384 * t + 384] = both.astype(BF16)

    def unpack(self, k, t, xl):
        upper = lax.broadcasted_iota(jnp.int32, (8, 384), 0) < 4
        upper1 = upper[:, :128]

        def swapped(v):
            return pltpu.roll(v, 4, 0)

        def unit(i, carry):
            z, q = i // 2, i % 2
            rows, more = [], []
            for p in (0, 1):
                a, b = (self.wp[k, z, xl, 4 * q + 2 * p + n, :, ds128(384 * t, 384)].astype(F32) for n in (0, 1))
                a0, a1, b0, b1 = a[:8], a[8:], b[:8], b[8:]
                rows += [a0, jnp.where(upper, a1, swapped(b0)), swapped(jnp.where(upper, b1, b0))]
                ea, eb = ([v[:, 128 * n : 128 * n + 128] for n in range(3)] for v in (a1, b1))
                more += [jnp.where(upper1, swapped(ea[0]), ea[1]), jnp.where(upper1, swapped(ea[2]), eb[0]),
                         jnp.where(upper1, swapped(eb[1]), eb[2])]
            self.w[k, z, xl, q, :, ds128(512 * t, 384)] = jnp.concatenate(rows, axis=0).astype(BF16)
            self.w[k, z, xl, q, :, ds128(512 * t + 384)] = jnp.concatenate(more, axis=0).astype(BF16)
            return carry

        lax.fori_loop(0, 16, unit, 0)

    def first_start(self, k):
        h = self.here
        src = self.own(k, 1)

        def peer(d):
            return {"y": (h.y + d * (1 - h.core)) % 8, "z": (h.z + d * h.core) % 8}

        order = (4, 3, 5, 2, 6, 1, 7)
        for d in order:
            remote(src, src, self.s1.at[k, 1], self.r1.at[k, 1], peer(d)).start()

        @pl.when(h.xl == h.core)
        def _():
            src = self.own(k, 0)
            for d in order + (0,):
                remote(src, src, self.s1x.at[k], self.r1.at[k, 0], {**h.on_x(1), **peer(d)}).start()
                if d:
                    remote(src, src, self.s1.at[k, 0], self.r1.at[k, 0], peer(d)).start()

    def first_wait(self, c, k, cls):
        h = self.here

        def wait(n):
            ref = self.blocks(k, n)
            remote(ref, ref, self.s1.at[k, cls], self.r1.at[k, cls], {"core": 1 - c}).wait_recv()

        if cls:
            wait(7)
        else:
            pl.when(h.xl == c)(lambda: wait(7))
            pl.when(h.xl != c)(lambda: wait(8))

    def to_core(self, c, k, which, step):
        src = self.chunk(c, k, min(which, 1), step, which == 2)
        remote(src, src, self.s4.at[k, which], self.r4.at[k, which], {"core": 1 - c}).start()

    def hop(self, c, k, cls, step):
        src = self.chunk(c, k, cls, step)
        far = 4 if cls == 1 else 3
        dirs = []
        if step <= 0 and 1 - step <= far:
            dirs.append((1, 1 - step))
        if step >= 0 and 1 + step <= 7 - far:
            dirs.append((-1, 1 + step))
        for way, nth in dirs:
            n = 0 if way == 1 else 1
            remote(src, src, self.s2.at[k, cls, n], self.r2.at[k, cls, n, nth],
                   self.here.along(c, way)).start()
        if cls == 1:
            far_x = (1 if step < 0 else -1) * (-1 if c == 1 and step in (0, -4) else 1)
            remote(src, src, self.s3.at[k], self.r3.at[k, step % 8], self.here.on_x(far_x)).start()
        self.to_core(c, k, cls, step)

    def second_start(self, c, k):
        for cls in (1, 0):
            self.first_wait(c, k, cls)
            self.hop(c, k, cls, 0)

    def second_step(self, c, k, nth):
        for cls in (1, 0):
            far = 4 if cls == 1 else 3
            for way in (1, -1):
                if nth > (far if way == 1 else 7 - far):
                    continue
                n = 0 if way == 1 else 1
                src = self.chunk(c, k, cls, -nth * way)
                remote(src, src, self.s2.at[k, cls, n], self.r2.at[k, cls, n, nth],
                       self.here.along(c, way)).wait_recv()
                self.hop(c, k, cls, -nth * way)
        self.cross_x(c, k, nth - 1)

    def cross_x(self, c, k, nth):
        for step in ((0,) if nth == 0 else (nth, -nth) if nth < 4 else (-4,)):
            src = self.chunk(c, k, 1, step, True)
            remote(src, src, self.s3.at[k], self.r3.at[k, step % 8], self.here.on_x(1)).wait_recv()
            self.to_core(c, k, 2, step)

    def from_core(self, k, which):
        ref = self.chunks(k, 8)
        remote(ref, ref, self.s4.at[k, which], self.r4.at[k, which], {"core": 1 - self.here.core}).wait_recv()

    def sent(self, k):
        h = self.here

        def wait(ref, sem, spare):
            remote(ref, ref, sem, spare, {"core": 1 - h.core}).wait_send()

        wait(self.blocks(k, 7), self.s1.at[k, 1], self.r1.at[k, 1])

        @pl.when(h.xl == h.core)
        def _():
            wait(self.blocks(k, 7), self.s1.at[k, 0], self.r1.at[k, 0])
            wait(self.blocks(k, 8), self.s1x.at[k], self.r1.at[k, 0])

        for cls in range(2):
            far = 4 if cls == 1 else 3
            for n in range(2):
                wait(self.chunks(k, far if n == 0 else 7 - far), self.s2.at[k, cls, n], self.r2.at[k, cls, n, 1])
        wait(self.chunks(k, 8), self.s3.at[k], self.r3.at[k, 0])
        for which in range(3):
            wait(self.chunks(k, 8), self.s4.at[k, which], self.r4.at[k, which])


def weight_scratch():
    sem = pltpu.SemaphoreType.DMA
    return [
        pltpu.VMEM((2, 8, 2, 2, 48, C), BF16),
        pltpu.VMEM((2, 8, 2, 8, 16, 1152), BF16),
        sem((2, 2)), sem((2, 2)), sem((2,)),
        sem((2, 2, 2)), sem((2, 2, 2, 5)),
        sem((2,)), sem((2, 8)),
        sem((2, 3)), sem((2, 3)),
    ]


EPS = 1e-05
ROWS = 128


class Sum:
    def __init__(self, here, parts, got, send, recv):
        self.__dict__.update(locals())
        self.me = 2 * here.x + here.core

    def group(self, m):
        x = m // 2
        return {"xh": x // 2, "xl": x % 2, "core": m % 2}

    def copies(self, stage):
        h, out = self.here, []
        for d in (4, 3, 5, 2, 6, 1, 7):
            if stage in (0, 3):
                m = (self.me + d) % 8
                src = self.parts.at[stage, m if stage == 0 else 0]
                dst, to = self.got.at[stage, self.me], self.group(m)
            elif stage == 1:
                src, dst, to = self.parts.at[1, 0], self.got.at[1, h.y], {"y": (h.y + d) % 8}
            else:
                src, dst, to = self.parts.at[2, 0], self.got.at[2, h.z], {"z": (h.z + d) % 8}
            out.append(remote(src, dst, self.send.at[stage, d], self.recv.at[stage, d], to))
        return out

    def mine(self, stage):
        return self.here.y if stage == 1 else self.here.z if stage == 2 else self.me

    def start(self, stage):
        src = self.parts[0, self.me] if stage == 0 else self.parts[stage, 0]
        self.got[stage, self.mine(stage)] = src
        for c in self.copies(stage):
            c.start()

    def finish(self, stage):
        for c in self.copies(stage):
            c.wait_recv()
        if stage < 3:
            total = self.got[stage, 0]
            for n in range(1, 8):
                total = total + self.got[stage, n]
            self.parts[stage + 1, 0] = total

    def sent(self):
        for stage in range(4):
            for c in self.copies(stage):
                c.wait_send()


def sum_scratch():
    sem = pltpu.SemaphoreType.DMA
    return [pltpu.VMEM((4, 8, 8, 128), F32), pltpu.VMEM((4, 8, 8, 128), F32), sem((4, 8)), sem((4, 8))]


def picked(rows, cols, where):
    r = lax.broadcasted_iota(jnp.int32, (rows, cols), 0)
    c = lax.broadcasted_iota(jnp.int32, (rows, cols), 1)
    return where(r, c).astype(BF16)


def dot(a, b):
    return jnp.dot(a, b, preferred_element_type=F32)


def dot_t(a, b):
    return lax.dot_general(a, b, (((1,), (1,)), ((), ())), preferred_element_type=F32)


def before(x, first):
    row = lax.broadcasted_iota(jnp.int32, x.shape, 0)
    return jnp.where(row == 0, first, pltpu.roll(x, 1, 0))


def after(x, last):
    row = lax.broadcasted_iota(jnp.int32, x.shape, 0)
    return jnp.where(row == x.shape[0] - 1, last, pltpu.roll(x, x.shape[0] - 1, 0))


def kernel(coarse_hbm, skip_hbm, w_in, w_out, taps, gain, grad_hbm, block_out, dx_out, gk_out, gg_out, *scratch):
    (ca, sk, go, halo_out, halo_in, act, gp, skp, halo, nrm, dgelu, scale, gm, gc, mer, mix, dn,
     in_sem, hs, hr, gain_row) = scratch[:21]
    gain_row[...] = gain[...].reshape(1, C)
    here = Here()
    w = Weights(here, *scratch[21:32])
    total = Sum(here, *scratch[32:])
    seq = here.z * 16 + here.xl * 8 + here.y

    loads = [pltpu.make_async_copy(a, b, in_sem.at[n])
             for n, (a, b) in enumerate(((coarse_hbm, ca), (skip_hbm, sk), (grad_hbm, go)))]
    for c in loads:
        c.start()
    w.pack(w_out, w_in)
    enter(here)
    w.first_start(0)
    w.first_start(1)
    total.parts[0] = jnp.zeros((8, 8, 128), F32)

    for c in loads:
        c.wait()
    row = lax.broadcasted_iota(jnp.int32, (16, C), 0)
    for side in (0, 1):
        rows = jnp.zeros((16, C), F32)
        for n, (ref, last) in enumerate(((ca, 63), (sk, 127), (go, 127))):
            for s in (0, 1):
                if side == 0:
                    r = ref[s, last - 15 : last + 1, :].astype(F32)[15:16]
                else:
                    r = ref[s, 0:16, :].astype(F32)[0:1]
                rows = jnp.where(row == 4 * n + 2 * side + s, r, rows)
        halo_out[side] = rows.astype(BF16)

    def neighbour(step):
        s = (seq + step + 128) % 128
        return {"z": s // 16, "xl": s % 16 // 8, "y": s % 8}

    halos = [remote(halo_out.at[0], halo_in.at[0], hs.at[0], hr.at[0], neighbour(1)),
             remote(halo_out.at[1], halo_in.at[1], hs.at[1], hr.at[1], neighbour(-1))]
    for c in halos:
        c.start()


    def norm(x):
        x = x.astype(F32)
        centered = x - jnp.mean(x, axis=-1, keepdims=True)
        r = lax.rsqrt(jnp.mean(centered * centered, axis=-1, keepdims=True) + EPS)
        n = centered * r
        u = n * gain_row[...]
        half = 0.5 + 0.5 * lax.erf(u * 0.7071067811865476)
        return n, r, u, half

    def norm_rows(i):
        at = pl.ds(pl.multiple_of(16 * i, 16), 16)
        n, r, u, half = norm(ca[i // 4, pl.ds(pl.multiple_of(16 * (i % 4), 16), 16), :])
        nrm[at, :] = n
        scale[at, :] = jnp.broadcast_to(r, (16, 128))
        act[at, :] = (u * half).astype(BF16)
        dgelu[at, :] = half + u * (0.3989422804014327 * jnp.exp(-0.5 * u * u))

    lax.fori_loop(0, 4, lambda i, v: (norm_rows(i), v)[1], 0)
    for k in (0, 1):
        on_core(here, lambda c: w.second_start(c, k))
    lax.fori_loop(4, 8, lambda i, v: (norm_rows(i), v)[1], 0)

    for c in halos:
        c.wait_recv()
    left = jnp.where(seq > 0, halo_in[0].astype(F32), 0.0)
    right = jnp.where(seq < 127, halo_in[1].astype(F32), 0.0)
    halo[...] = (left + right).astype(BF16)
    gp[256:272, :] = halo[...]
    on_core(here, lambda c: w.second_step(c, 0, 1))
    on_core(here, lambda c: w.second_step(c, 1, 1))
    _, _, u, half = norm(halo[...])
    act[128:144, :] = (u * half).astype(BF16)
    split = picked(128, 128, lambda r, c: c == 2 * (r % 64) + r // 64)
    for s in (0, 1):
        gp[128 * s : 128 * s + 128, :] = dot(split, go[s]).astype(BF16)
        skp[128 * s : 128 * s + 128, :] = dot(split, sk[s]).astype(BF16)
    for nth in (2, 3, 4):
        for k in (0, 1):
            on_core(here, lambda c: w.second_step(c, k, nth))

    def mine(k):
        w.unpack(k, 1 + here.core, here.xl)
        w.unpack(k, 0, here.core)

    def crossed(k):
        on_core(here, lambda c: w.cross_x(c, k, 4))

    def theirs(k):
        w.unpack(k, 1 + here.core, 1 - here.xl)
        w.from_core(k, 0)
        w.unpack(k, 0, 1 - here.core)
        w.from_core(k, 1)
        w.unpack(k, 2 - here.core, here.xl)

    def last(k):
        w.from_core(k, 2)
        w.unpack(k, 2 - here.core, 1 - here.xl)

    def cols(n):
        return pl.ds(384 * n, 384)

    def back(n):
        at = cols(n)
        rows = w.w[0, pl.ds(2 * n, 2)].reshape(384, C)
        gm[:, at] = dot_t(gp[...], rows).astype(BF16)
        t0, t1, t2 = (taps[t : t + 1, at] for t in range(3))
        edge = gm[256:272, at].astype(F32)
        for s in (0, 1):
            e = gm[128 * s : 128 * s + 64, at].astype(F32)
            o = gm[128 * s + 64 : 128 * s + 128, at].astype(F32)
            e1 = after(e, edge[10 + s : 11 + s])
            o1 = before(o, edge[8 + s : 9 + s])
            gc[64 * s : 64 * s + 64, at] = (t0 * (o + e1) + t1 * (e + o) + t2 * (o1 + e)).astype(BF16)

    mine(0)
    crossed(0)
    mine(1)
    theirs(0)
    crossed(1)
    last(0)
    for n in range(4):
        back(n)
    theirs(1)
    last(1)

    def give(row, n, v):
        for i in range(3):
            m, at = 2 * row + n // 2, 3 * (n % 2) + i
            total.parts[0, m, at : at + 1, :] = v[:, 128 * i : 128 * i + 128]

    def forth(n):
        at = cols(n)
        co = dot(act[...], w.w[1, :, :, :, :, at].reshape(C, 384)).astype(BF16).astype(F32)
        t0, t1, t2 = (taps[t : t + 1, at] for t in range(3))
        skip_edge = halo[:, at].astype(F32)
        sums = [0.0, 0.0, 0.0]
        for s in (0, 1):
            c = co[64 * s : 64 * s + 64]
            me = (c + skp[128 * s : 128 * s + 64, at].astype(F32)).astype(BF16).astype(F32)
            mo = (c + skp[128 * s + 64 : 128 * s + 128, at].astype(F32)).astype(BF16).astype(F32)
            lo = (co[128 + s : 129 + s] + skip_edge[4 + s : 5 + s]).astype(BF16).astype(F32)
            hi = (co[130 + s : 131 + s] + skip_edge[6 + s : 7 + s]).astype(BF16).astype(F32)
            mo1 = before(mo, lo)
            me1 = after(me, hi)
            mix[128 * s : 128 * s + 64, at] = (t0 * mo1 + t1 * me + t2 * mo).astype(BF16)
            mix[128 * s + 64 : 128 * s + 128, at] = (t0 * me + t1 * mo + t2 * me1).astype(BF16)
            e = gm[128 * s : 128 * s + 64, at].astype(F32)
            o = gm[128 * s + 64 : 128 * s + 128, at].astype(F32)
            for t, v in enumerate((mo1 * e + me * o, me * e + mo * o, mo * e + me1 * o)):
                sums[t] = sums[t] + jnp.sum(v, axis=0, keepdims=True)
        for t in range(3):
            give(t, n, sums[t])

    for n in range(4):
        forth(n)

    def gains(n, sums):
        at = cols(n)
        ga = dot_t(gc[...], w.w[1, pl.ds(2 * n, 2)].reshape(384, C))
        gu = ga * dgelu[:, at]
        nn = nrm[:, at]
        give(3, n, jnp.sum(gu * nn, axis=0, keepdims=True))
        d = gu * gain_row[:, at]
        dn[:, at] = d
        return (sums[0] + jnp.sum(d, axis=1, keepdims=True), sums[1] + jnp.sum(d * nn, axis=1, keepdims=True))

    sums = (0.0, 0.0)
    for n in range(4):
        sums = gains(n, sums)
    d_sum, dn_sum = sums

    total.start(0)

    d_mean, dn_mean = d_sum / C, dn_sum / C
    for n in range(4):
        at = pl.ds(384 * n, 384)
        v = scale[:, 0:1] * (dn[:, at] - d_mean - nrm[:, at] * dn_mean)
        for s in (0, 1):
            dx_out[s, :, at] = v[64 * s : 64 * s + 64].astype(BF16)
    total.finish(0)
    total.start(1)
    join = picked(128, 128, lambda r, c: r == 2 * (c % 64) + c // 64)
    for s in (0, 1):
        mer[128 * s : 128 * s + 128, :] = dot(join, mix[128 * s : 128 * s + 128, :]).astype(BF16)

    def final(n):
        at = cols(n)
        v = dot(mer[...], w.w[0, :, :, :, :, at].reshape(C, 384)).astype(BF16)
        for s in (0, 1):
            block_out[s, :, at] = v[128 * s : 128 * s + 128]

    final(0)
    final(1)
    total.finish(1)
    total.start(2)
    final(2)
    final(3)
    total.finish(2)
    total.start(3)
    for k in (0, 1):
        w.sent(k)
    for c in halos:
        c.wait_send()
    total.finish(3)
    total.sent()
    for m in range(8):
        r, at = m // 2, 768 * (m % 2)
        for i in range(6):
            v = total.got[3, m, i : i + 1, :]
            if r < 3:
                gk_out[r : r + 1, at + 128 * i : at + 128 * i + 128] = v
            else:
                gg_out[at + 128 * i : at + 128 * i + 128] = v[0]


def on_device(coarse_act, skip_act, proj_in, proj_out, depth_kernel, norm_gain, grad_out):
    vmem = pl.BlockSpec(memory_space=pltpu.VMEM)
    hbm = pl.BlockSpec(memory_space=pl.ANY)
    sem = pltpu.SemaphoreType.DMA

    def b(*shape):
        return pltpu.VMEM(shape, BF16)

    def f(*shape):
        return pltpu.VMEM(shape, F32)

    scratch = [
        b(2, 64, C), b(2, 128, C), b(2, 128, C), b(2, 16, C), b(2, 16, C), b(144, C), b(272, C), b(256, C), b(16, C),
        f(ROWS, C), f(ROWS, C), f(ROWS, 128), b(272, C), b(ROWS, C), b(256, C), b(256, C), f(ROWS, C),
        sem((3,)), sem((2,)), sem((2,)), f(1, C),
    ] + weight_scratch() + sum_scratch()
    block, dx, gk, gg = pl.pallas_call(
        kernel,
        out_shape=(
            pltpu.VMEM((2, 128, C), BF16), pltpu.VMEM((2, 64, C), BF16), pltpu.VMEM((3, C), F32), pltpu.VMEM((C,), F32)),
        in_specs=[hbm, hbm, vmem, vmem, vmem, vmem, hbm],
        out_specs=(vmem,) * 4,
        scratch_shapes=scratch,
        compiler_params=pltpu.CompilerParams(collective_id=0, has_side_effects=True, vmem_limit_bytes=62 << 20),
        cost_estimate=pl.CostEstimate(flops=3700000000, bytes_accessed=4000000, transcendentals=400000),
    )(coarse_act, skip_act, proj_in, proj_out, depth_kernel, norm_gain, grad_out)
    return hand_over(block, dx, gk, gg)


def hand_over(*arrays):
    def body(*refs):
        sem = refs[8]
        pairs = []
        for n in range(4):
            src, dst = refs[n], refs[4 + n]
            if n < 2:
                half = src.shape[1] // 2
                for s in (0, 1):
                    for q in (0, 1):
                        at = (s, pl.ds(half * q, half))
                        pairs.append((src.at[at], dst.at[at]))
            else:
                pairs.append((src, dst))
        copies = [pltpu.make_async_copy(a, d, sem.at[n]) for n, (a, d) in enumerate(pairs)]
        for c in copies:
            c.start()
        for c in copies:
            c.wait()

    arrays = [pltpu.with_memory_space_constraint(a, pltpu.VMEM) for a in arrays]
    return pl.pallas_call(
        body, out_shape=tuple(jax.ShapeDtypeStruct(s, d) for s, d in (
            ((2, 128, C), BF16), ((2, 64, C), BF16), ((3, C), F32), ((C,), F32))),
        in_specs=[pl.BlockSpec(memory_space=pltpu.VMEM)] * 4, out_specs=(pl.BlockSpec(memory_space=pl.ANY),) * 4,
        scratch_shapes=[pltpu.SemaphoreType.DMA((10,))],
        compiler_params=pltpu.CompilerParams(vmem_limit_bytes=60 << 20),
    )(*arrays)


def solution(mesh):
    split = Mesh(mesh.devices.reshape(8, 2, 8, 2, 2), AXES)
    seq, batch = ("z", "xl", "y"), ("xh", "core")
    big, rows = P(batch, seq, None), P(seq, None)
    return jax.shard_map(
        on_device, mesh=split, in_specs=(big, big, rows, rows, P(), P(), big),
        out_specs=(big, big, P(), P()), check_vma=False)
```

```python
import functools
import jax
import jax.numpy as jnp
from jax import lax
from jax.experimental import pallas as pl
from jax.experimental.pallas import tpu as pltpu
from jax.sharding import Mesh
from jax.sharding import PartitionSpec as P

AXES = ("z", "xl", "y", "xh", "core")
F32 = jnp.float32
BF16 = jnp.bfloat16
C = 1536


def remote(src, dst, send, recv, dev):
    return pltpu.make_async_remote_copy(
        src_ref=src, dst_ref=dst, send_sem=send, recv_sem=recv,
        device_id=dev, device_id_type=pl.DeviceIdType.MESH)


def ds128(i, n=128):
    return pl.ds(pl.multiple_of(i, 128), n)


class Here:
    def __init__(self):
        for a in AXES:
            setattr(self, a, lax.axis_index(a))
        self.x = 2 * self.xh + self.xl

    def on_x(self, step):
        x = (self.x + step + 4) % 4
        return {"xh": x // 2, "xl": x % 2}

    def along(self, core, step):
        name = "z" if core == 0 else "y"
        return {name: (getattr(self, name) + step + 8) % 8}


def on_core(here, f):
    for c in (0, 1):
        @pl.when(here.core == c)
        def _(c=c):
            f(c)


def greet(here):
    barrier = pltpu.get_barrier_semaphore()
    peers = []
    for d in range(1, 8):
        peers.append({"y": (here.y + d) % 8})
        peers.append({"z": (here.z + d) % 8})
        for step in (1, -1):
            peers.append({**here.on_x(step), "y": (here.y + d * (1 - here.core)) % 8, "z": (here.z + d * here.core) % 8})
    for d in range(4):
        for e in range(2):
            if d or e:
                peers.append({**here.on_x(d), "core": (here.core + e) % 2})
    seq = here.z * 16 + here.xl * 8 + here.y
    for step in (1, 127):
        n = (seq + step) % 128
        peers.append({"z": n // 16, "xl": n % 16 // 8, "y": n % 8})
    for p in peers:
        pl.semaphore_signal(barrier, inc=1, device_id=p, device_id_type=pl.DeviceIdType.MESH)
    return lambda: pl.semaphore_wait(barrier, len(peers))


class Weights:
    def __init__(self, here, w, wp, s1, r1, s1x, s2, r2, s3, r3, s4, r4):
        self.__dict__.update(locals())

    def own(self, k, cls):
        h = self.here
        t = 1 + h.core if cls else 0
        return self.wp.at[k, t, h.z, h.xl, h.y]

    def chunk(self, c, k, cls, step, other=False):
        h = self.here
        t, xl = (0, c) if cls == 0 else (1 + c, (1 - h.xl) if other else h.xl)
        if c == 0:
            return self.wp.at[k, t, (h.z + step + 8) % 8, xl]
        return self.wp.at[k, t, :, xl, (h.y + step + 8) % 8]

    def chunks(self, k, n):
        return self.wp.at[k, 0, pl.ds(0, n), 0]

    def blocks(self, k, n):
        return self.wp.at[k, 0, 0, 0, pl.ds(0, n)]

    def pack(self, *refs):
        h = self.here

        def one(k, ref, t):
            v = ref[:, ds128(512 * t, 512)].astype(F32)
            e = v[:, 384:]
            low = jnp.concatenate([e[0:4], e[4:8], e[8:12]], axis=1)
            self.wp[k, t, h.z, h.xl, h.y] = jnp.concatenate([v[:, :384], low], axis=0).astype(BF16)

        for k, ref in enumerate(refs):
            one(k, ref, 1 + h.core)

        @pl.when(h.xl == h.core)
        def _():
            for k, ref in enumerate(refs):
                one(k, ref, 0)

    def unpack(self, k, t, xl):
        upper = lax.broadcasted_iota(jnp.int32, (8, 384), 0) < 4
        upper1 = upper[:, :128]

        def swapped(v):
            return pltpu.roll(v, 4, 0)

        def unit(i, carry):
            z, q = i // 2, i % 2
            rows, more = [], []
            for p in (0, 1):
                a, b = (self.wp[k, t, z, xl, 4 * q + 2 * p + n].astype(F32) for n in (0, 1))
                a0, a1, b0, b1 = a[:8], a[8:], b[:8], b[8:]
                rows += [a0, jnp.where(upper, a1, swapped(b0)), swapped(jnp.where(upper, b1, b0))]
                ea, eb = ([v[:, 128 * n : 128 * n + 128] for n in range(3)] for v in (a1, b1))
                more += [jnp.where(upper1, swapped(ea[0]), ea[1]), jnp.where(upper1, swapped(ea[2]), eb[0]),
                         jnp.where(upper1, swapped(eb[1]), eb[2])]
            at = pl.ds(pl.multiple_of(192 * z + 96 * xl + 48 * q, 16), 48)
            self.w[k, at, ds128(512 * t, 384)] = jnp.concatenate(rows, axis=0).astype(BF16)
            self.w[k, at, ds128(512 * t + 384)] = jnp.concatenate(more, axis=0).astype(BF16)
            return carry

        lax.fori_loop(0, 16, unit, 0, unroll=4)

    def first_start(self, k, cls):
        h = self.here
        src = self.own(k, cls)

        def peer(d):
            return {"y": (h.y + d * (1 - h.core)) % 8, "z": (h.z + d * h.core) % 8}

        def send(d):
            remote(src, src, self.s1.at[k, cls], self.r1.at[k, cls], peer(d)).start()

        order = (4, 3, 5, 2, 6, 1, 7)
        if cls:
            for d in order:
                send(d)
            return

        @pl.when(h.xl == h.core)
        def _():
            for d in order + (0,):
                remote(src, src, self.s1x.at[k], self.r1.at[k, 0], {**h.on_x(1), **peer(d)}).start()
                if d:
                    send(d)

    def first_wait(self, c, k, cls):
        h = self.here

        def wait(n):
            ref = self.blocks(k, n)
            remote(ref, ref, self.s1.at[k, cls], self.r1.at[k, cls], {"core": 1 - c}).wait_recv()

        if cls:
            wait(7)
        else:
            pl.when(h.xl == c)(lambda: wait(7))
            pl.when(h.xl != c)(lambda: wait(8))

    def to_core(self, c, k, which, step):
        src = self.chunk(c, k, min(which, 1), step, which == 2)
        remote(src, src, self.s4.at[k, which], self.r4.at[k, which], {"core": 1 - c}).start()

    def hop(self, c, k, cls, step):
        src = self.chunk(c, k, cls, step)
        far = 4 if cls == 1 else 3
        dirs = []
        if step <= 0 and 1 - step <= far:
            dirs.append((1, 1 - step))
        if step >= 0 and 1 + step <= 7 - far:
            dirs.append((-1, 1 + step))
        for way, nth in dirs:
            n = 0 if way == 1 else 1
            remote(src, src, self.s2.at[k, cls, n], self.r2.at[k, cls, n, nth],
                   self.here.along(c, way)).start()
        if cls == 1:
            far_x = (1 if step < 0 else -1) * (-1 if c == 1 and step in (0, -4) else 1)
            remote(src, src, self.s3.at[k], self.r3.at[k, step % 8], self.here.on_x(far_x)).start()
        self.to_core(c, k, cls, step)

    def second_step(self, c, k, cls, nth):
        if nth == 0:
            self.first_wait(c, k, cls)
            self.hop(c, k, cls, 0)
            return
        far = 4 if cls == 1 else 3
        for way in (1, -1):
            if nth > (far if way == 1 else 7 - far):
                continue
            n = 0 if way == 1 else 1
            src = self.chunk(c, k, cls, -nth * way)
            remote(src, src, self.s2.at[k, cls, n], self.r2.at[k, cls, n, nth],
                   self.here.along(c, way)).wait_recv()
            self.hop(c, k, cls, -nth * way)
        if cls:
            self.cross_x(c, k, nth - 1)

    def cross_x(self, c, k, nth):
        for step in ((0,) if nth == 0 else (nth, -nth) if nth < 4 else (-4,)):
            src = self.chunk(c, k, 1, step, True)
            remote(src, src, self.s3.at[k], self.r3.at[k, step % 8], self.here.on_x(1)).wait_recv()
            self.to_core(c, k, 2, step)

    def from_core(self, k, which):
        ref = self.chunks(k, 8)
        remote(ref, ref, self.s4.at[k, which], self.r4.at[k, which], {"core": 1 - self.here.core}).wait_recv()

    def sent(self, k):
        h = self.here

        def wait(ref, sem, spare):
            remote(ref, ref, sem, spare, {"core": 1 - h.core}).wait_send()

        wait(self.blocks(k, 7), self.s1.at[k, 1], self.r1.at[k, 1])

        @pl.when(h.xl == h.core)
        def _():
            wait(self.blocks(k, 7), self.s1.at[k, 0], self.r1.at[k, 0])
            wait(self.blocks(k, 8), self.s1x.at[k], self.r1.at[k, 0])

        for cls in range(2):
            far = 4 if cls == 1 else 3
            for n in range(2):
                wait(self.chunks(k, far if n == 0 else 7 - far), self.s2.at[k, cls, n], self.r2.at[k, cls, n, 1])
        wait(self.chunks(k, 8), self.s3.at[k], self.r3.at[k, 0])
        for which in range(3):
            wait(self.chunks(k, 8), self.s4.at[k, which], self.r4.at[k, which])


def weight_scratch():
    sem = pltpu.SemaphoreType.DMA
    return [
        pltpu.VMEM((2, C, C), BF16),
        pltpu.VMEM((2, 3, 8, 2, 8, 16, 384), BF16),
        sem((2, 2)), sem((2, 2)), sem((2,)),
        sem((2, 2, 2)), sem((2, 2, 2, 5)),
        sem((2,)), sem((2, 8)),
        sem((2, 3)), sem((2, 3)),
    ]


EPS = 1e-05
ROWS = 128


class Sum:
    def __init__(self, here, parts, got, send, recv):
        self.__dict__.update(locals())
        self.me = 2 * here.x + here.core

    def group(self, m):
        x = m // 2
        return {"xh": x // 2, "xl": x % 2, "core": m % 2}

    def copies(self, stage):
        h, out = self.here, []
        for d in (4, 3, 5, 2, 6, 1, 7):
            if stage in (0, 3):
                m = (self.me + d) % 8
                src = self.parts.at[stage, m if stage == 0 else 0]
                dst, to = self.got.at[stage, self.me], self.group(m)
            elif stage == 1:
                src, dst, to = self.parts.at[1, 0], self.got.at[1, h.y], {"y": (h.y + d) % 8}
            else:
                src, dst, to = self.parts.at[2, 0], self.got.at[2, h.z], {"z": (h.z + d) % 8}
            out.append(remote(src, dst, self.send.at[stage, d], self.recv.at[stage, d], to))
        return out

    def mine(self, stage):
        return self.here.y if stage == 1 else self.here.z if stage == 2 else self.me

    def start(self, stage):
        src = self.parts[0, self.me] if stage == 0 else self.parts[stage, 0]
        self.got[stage, self.mine(stage)] = src
        for c in self.copies(stage):
            c.start()

    def finish(self, stage):
        for c in self.copies(stage):
            c.wait_recv()
        if stage < 3:
            total = self.got[stage, 0]
            for n in range(1, 8):
                total = total + self.got[stage, n]
            self.parts[stage + 1, 0] = total

    def sent(self, *stages):
        for stage in stages:
            for c in self.copies(stage):
                c.wait_send()


def sum_scratch():
    sem = pltpu.SemaphoreType.DMA
    return [pltpu.VMEM((4, 8, 8, 128), F32), pltpu.VMEM((4, 8, 8, 128), F32), sem((4, 8)), sem((4, 8))]


def picked(rows, cols, where):
    r = lax.broadcasted_iota(jnp.int32, (rows, cols), 0)
    c = lax.broadcasted_iota(jnp.int32, (rows, cols), 1)
    return where(r, c).astype(BF16)


def dot(a, b):
    return jnp.dot(a, b, preferred_element_type=F32)


def dot_t(a, b):
    return lax.dot_general(a, b, (((1,), (1,)), ((), ())), preferred_element_type=F32)


def before(x, first):
    row = lax.broadcasted_iota(jnp.int32, x.shape, 0)
    return jnp.where(row == 0, first, pltpu.roll(x, 1, 0))


def after(x, last):
    row = lax.broadcasted_iota(jnp.int32, x.shape, 0)
    return jnp.where(row == x.shape[0] - 1, last, pltpu.roll(x, x.shape[0] - 1, 0))


def kernel(coarse_hbm, skip_hbm, in_hbm, out_hbm, taps_hbm, gain_hbm, grad_hbm, block_out, dx_out, gk_out, gg_out, *scratch):
    (ca, sk, go, halo_out, halo_in, act, gp, skp, halo, nrm, dgelu, scale, gm, gc, mer, mix, dn,
     in_sem, hs, hr, gain_row, w_in, w_out, taps, gain) = scratch[:25]
    here = Here()
    w = Weights(here, *scratch[25:36])
    total = Sum(here, *scratch[36:])
    seq = here.z * 16 + here.xl * 8 + here.y

    loads = [pltpu.make_async_copy(a, b, in_sem.at[n]) for n, (a, b) in enumerate((
        (out_hbm, w_out), (in_hbm, w_in), (coarse_hbm, ca), (skip_hbm, sk), (grad_hbm, go), (taps_hbm, taps),
        (gain_hbm, gain)))]
    for c in loads:
        c.start()
    all_here = greet(here)
    for c in loads[:2]:
        c.wait()
    w.pack(w_out, w_in)
    all_here()
    for cls, k in ((1, 0), (0, 0), (1, 1), (0, 1)):
        w.first_start(k, cls)
    total.parts[0] = jnp.zeros((8, 8, 128), F32)

    def ring(*steps):
        for cls, k, nth in steps:
            on_core(here, lambda c: w.second_step(c, k, cls, nth))

    for c in loads[2:]:
        c.wait()
    gain_row[...] = gain[...].reshape(1, C)
    row = lax.broadcasted_iota(jnp.int32, (16, C), 0)
    for side in (0, 1):
        rows = jnp.zeros((16, C), F32)
        for n, (ref, last) in enumerate(((ca, 63), (sk, 127), (go, 127))):
            for s in (0, 1):
                if side == 0:
                    r = ref[s, last - 15 : last + 1, :].astype(F32)[15:16]
                else:
                    r = ref[s, 0:16, :].astype(F32)[0:1]
                rows = jnp.where(row == 4 * n + 2 * side + s, r, rows)
        halo_out[side] = rows.astype(BF16)

    def neighbour(step):
        s = (seq + step + 128) % 128
        return {"z": s // 16, "xl": s % 16 // 8, "y": s % 8}

    halos = [remote(halo_out.at[0], halo_in.at[0], hs.at[0], hr.at[0], neighbour(1)),
             remote(halo_out.at[1], halo_in.at[1], hs.at[1], hr.at[1], neighbour(-1))]
    for c in halos:
        c.start()


    def norm(x):
        x = x.astype(F32)
        centered = x - jnp.mean(x, axis=-1, keepdims=True)
        r = lax.rsqrt(jnp.mean(centered * centered, axis=-1, keepdims=True) + EPS)
        n = centered * r
        u = n * gain_row[...]
        half = 0.5 + 0.5 * lax.erf(u * 0.7071067811865476)
        return n, r, u, half

    def norm_rows(i):
        at = pl.ds(pl.multiple_of(16 * i, 16), 16)
        n, r, u, half = norm(ca[i // 4, pl.ds(pl.multiple_of(16 * (i % 4), 16), 16), :])
        nrm[at, :] = n
        scale[at, :] = jnp.broadcast_to(r, (16, 128))
        act[at, :] = (u * half).astype(BF16)
        dgelu[at, :] = half + u * (0.3989422804014327 * jnp.exp(-0.5 * u * u))

    lax.fori_loop(0, 4, lambda i, v: (norm_rows(i), v)[1], 0)
    ring((1, 0, 0), (0, 0, 0), (1, 1, 0), (0, 1, 0))
    lax.fori_loop(4, 8, lambda i, v: (norm_rows(i), v)[1], 0)

    for c in halos:
        c.wait_recv()
    left = jnp.where(seq > 0, halo_in[0].astype(F32), 0.0)
    right = jnp.where(seq < 127, halo_in[1].astype(F32), 0.0)
    halo[...] = (left + right).astype(BF16)
    gp[256:272, :] = halo[...]
    ring((1, 0, 1), (0, 0, 1), (1, 1, 1), (0, 1, 1))
    _, _, u, half = norm(halo[...])
    act[128:144, :] = (u * half).astype(BF16)
    split = picked(128, 128, lambda r, c: c == 2 * (r % 64) + r // 64)
    for s in (0, 1):
        gp[128 * s : 128 * s + 128, :] = dot(split, go[s]).astype(BF16)
        skp[128 * s : 128 * s + 128, :] = dot(split, sk[s]).astype(BF16)
    for nth in (2, 3):
        ring((1, 0, nth), (0, 0, nth), (1, 1, nth), (0, 1, nth))
    ring((1, 0, 4), (0, 0, 4), (1, 1, 4), (0, 1, 4))

    def crossed(k):
        on_core(here, lambda c: w.cross_x(c, k, 4))

    def theirs(k):
        w.unpack(k, 1 + here.core, 1 - here.xl)
        w.from_core(k, 0)
        w.unpack(k, 0, 1 - here.core)
        w.from_core(k, 1)
        w.unpack(k, 2 - here.core, here.xl)

    def last(k):
        w.from_core(k, 2)
        w.unpack(k, 2 - here.core, 1 - here.xl)

    def cols(n):
        return pl.ds(512 * n, 512)

    def back(n):
        at = cols(n)
        rows = w.w[0, cols(n), :]
        gm[:, at] = dot_t(gp[...], rows).astype(BF16)
        t0, t1, t2 = (taps[t : t + 1, at] for t in range(3))
        edge = gm[256:272, at].astype(F32)
        for s in (0, 1):
            e = gm[128 * s : 128 * s + 64, at].astype(F32)
            o = gm[128 * s + 64 : 128 * s + 128, at].astype(F32)
            e1 = after(e, edge[10 + s : 11 + s])
            o1 = before(o, edge[8 + s : 9 + s])
            gc[64 * s : 64 * s + 64, at] = (t0 * (o + e1) + t1 * (e + o) + t2 * (o1 + e)).astype(BF16)

    w.unpack(0, 1 + here.core, here.xl)
    w.unpack(0, 0, here.core)
    crossed(0)
    w.unpack(1, 1 + here.core, here.xl)
    w.unpack(1, 0, here.core)
    theirs(0)
    last(0)
    back(0)
    crossed(1)
    back(1)
    back(2)
    theirs(1)
    last(1)

    def give(row, n, v):
        for i in range(4):
            m, at = (12 * row + 4 * n + i) // 6, (12 * row + 4 * n + i) % 6
            total.parts[0, m, at : at + 1, :] = v[:, 128 * i : 128 * i + 128]

    def forth(n):
        at = cols(n)
        co = dot(act[...], w.w[1, :, at]).astype(BF16).astype(F32)
        t0, t1, t2 = (taps[t : t + 1, at] for t in range(3))
        skip_edge = halo[:, at].astype(F32)
        sums = [0.0, 0.0, 0.0]
        for s in (0, 1):
            c = co[64 * s : 64 * s + 64]
            me = (c + skp[128 * s : 128 * s + 64, at].astype(F32)).astype(BF16).astype(F32)
            mo = (c + skp[128 * s + 64 : 128 * s + 128, at].astype(F32)).astype(BF16).astype(F32)
            lo = (co[128 + s : 129 + s] + skip_edge[4 + s : 5 + s]).astype(BF16).astype(F32)
            hi = (co[130 + s : 131 + s] + skip_edge[6 + s : 7 + s]).astype(BF16).astype(F32)
            mo1 = before(mo, lo)
            me1 = after(me, hi)
            mix[128 * s : 128 * s + 64, at] = (t0 * mo1 + t1 * me + t2 * mo).astype(BF16)
            mix[128 * s + 64 : 128 * s + 128, at] = (t0 * me + t1 * mo + t2 * me1).astype(BF16)
            e = gm[128 * s : 128 * s + 64, at].astype(F32)
            o = gm[128 * s + 64 : 128 * s + 128, at].astype(F32)
            for t, v in enumerate((mo1 * e + me * o, me * e + mo * o, mo * e + me1 * o)):
                sums[t] = sums[t] + jnp.sum(v, axis=0, keepdims=True)
        for t in range(3):
            give(t, n, sums[t])

    for n in range(3):
        forth(n)

    def gains(n, sums):
        at = cols(n)
        ga = dot_t(gc[...], w.w[1, at, :])
        gu = ga * dgelu[:, at]
        nn = nrm[:, at]
        give(3, n, jnp.sum(gu * nn, axis=0, keepdims=True))
        d = gu * gain_row[:, at]
        dn[:, at] = d
        return (sums[0] + jnp.sum(d, axis=1, keepdims=True), sums[1] + jnp.sum(d * nn, axis=1, keepdims=True))

    sums = (0.0, 0.0)
    for n in range(3):
        sums = gains(n, sums)
    d_sum, dn_sum = sums

    total.start(0)

    d_mean, dn_mean = d_sum / C, dn_sum / C
    for n in range(3):
        at = cols(n)
        v = scale[:, 0:1] * (dn[:, at] - d_mean - nrm[:, at] * dn_mean)
        for s in (0, 1):
            dx_out[s, :, at] = v[64 * s : 64 * s + 64].astype(BF16)
    total.finish(0)
    total.start(1)
    join = picked(128, 128, lambda r, c: r == 2 * (c % 64) + c // 64)
    for s in (0, 1):
        mer[128 * s : 128 * s + 128, :] = dot(join, mix[128 * s : 128 * s + 128, :]).astype(BF16)

    def final(n):
        at = cols(n)
        v = dot(mer[...], w.w[0, :, at]).astype(BF16)
        for s in (0, 1):
            block_out[s, :, at] = v[128 * s : 128 * s + 128]

    final(0)
    total.finish(1)
    total.start(2)
    final(1)
    final(2)
    total.finish(2)
    total.start(3)
    for k in (0, 1):
        w.sent(k)
    for c in halos:
        c.wait_send()
    total.sent(0, 1, 2)
    total.finish(3)
    total.sent(3)
    for m in range(8):
        r, at = m // 2, 768 * (m % 2)
        for i in range(6):
            v = total.got[3, m, i : i + 1, :]
            if r < 3:
                gk_out[r : r + 1, at + 128 * i : at + 128 * i + 128] = v
            else:
                gg_out[at + 128 * i : at + 128 * i + 128] = v[0]


def on_device(coarse_act, skip_act, proj_in, proj_out, depth_kernel, norm_gain, grad_out):
    vmem = pl.BlockSpec(memory_space=pltpu.VMEM)
    hbm = pl.BlockSpec(memory_space=pl.ANY)
    sem = pltpu.SemaphoreType.DMA

    def b(*shape):
        return pltpu.VMEM(shape, BF16)

    def f(*shape):
        return pltpu.VMEM(shape, F32)

    scratch = [
        b(2, 64, C), b(2, 128, C), b(2, 128, C), b(2, 16, C), b(2, 16, C), b(144, C), b(272, C), b(256, C), b(16, C),
        f(ROWS, C), f(ROWS, C), f(ROWS, 128), b(272, C), b(ROWS, C), b(256, C), b(256, C), f(ROWS, C),
        sem((7,)), sem((2,)), sem((2,)), f(1, C), b(12, C), b(12, C), f(3, C), f(C),
    ] + weight_scratch() + sum_scratch()
    block, dx, gk, gg = pl.pallas_call(
        kernel,
        out_shape=(
            pltpu.VMEM((2, 128, C), BF16), pltpu.VMEM((2, 64, C), BF16), pltpu.VMEM((3, C), F32), pltpu.VMEM((C,), F32)),
        in_specs=[hbm] * 7,
        out_specs=(vmem,) * 4,
        scratch_shapes=scratch,
        compiler_params=pltpu.CompilerParams(collective_id=0, has_side_effects=True, vmem_limit_bytes=62 << 20),
        cost_estimate=pl.CostEstimate(flops=3700000000, bytes_accessed=4000000, transcendentals=400000),
    )(coarse_act, skip_act, proj_in, proj_out, depth_kernel, norm_gain, grad_out)
    return hand_over(block, dx, gk, gg)


def hand_over(*arrays):
    def body(*refs):
        sem = refs[8]
        pairs = []
        for n in range(4):
            src, dst = refs[n], refs[4 + n]
            if n < 2:
                half = src.shape[1] // 2
                for s in (0, 1):
                    for q in (0, 1):
                        at = (s, pl.ds(half * q, half))
                        pairs.append((src.at[at], dst.at[at]))
            else:
                pairs.append((src, dst))
        copies = [pltpu.make_async_copy(a, d, sem.at[n]) for n, (a, d) in enumerate(pairs)]
        for c in copies:
            c.start()
        for c in copies:
            c.wait()

    arrays = [pltpu.with_memory_space_constraint(a, pltpu.VMEM) for a in arrays]
    return pl.pallas_call(
        body, out_shape=tuple(jax.ShapeDtypeStruct(s, d) for s, d in (
            ((2, 128, C), BF16), ((2, 64, C), BF16), ((3, C), F32), ((C,), F32))),
        in_specs=[pl.BlockSpec(memory_space=pltpu.VMEM)] * 4, out_specs=(pl.BlockSpec(memory_space=pl.ANY),) * 4,
        scratch_shapes=[pltpu.SemaphoreType.DMA((10,))],
        compiler_params=pltpu.CompilerParams(vmem_limit_bytes=60 << 20),
    )(*arrays)


def solution(mesh):
    split = Mesh(mesh.devices.reshape(8, 2, 8, 2, 2), AXES)
    seq, batch = ("z", "xl", "y"), ("xh", "core")
    big, rows = P(batch, seq, None), P(seq, None)
    return jax.shard_map(
        on_device, mesh=split, in_specs=(big, big, rows, rows, P(), P(), big),
        out_specs=(big, big, P(), P()), check_vma=False)
```
